256 devices in a mesh: ctx: 16 (over x_hi, z), head: 16 (over y, x_lo, core).
Axes of the slice: x: 4 (x_hi: 2, x_lo: 2; x = x_hi * 2 + x_lo), y: 4, z: 8, core: 2. Of those that a mesh axis runs over, the one named last changes fastest.
Arguments:
- mixer_in: bfloat16 [4096, 16384], P('ctx', 'head'), may hold values from -6 to 6
- gate_in: bfloat16 [4096, 16384], P('ctx', 'head'), may hold values from -6 to 6
- b_proj: bfloat16 [4096, 2048], P('ctx'), may hold values from -6 to 6
- c_proj: bfloat16 [4096, 2048], P('ctx'), may hold values from -0.375 to 0.375
- step_size: float32 [4096, 256], P('ctx', 'head')
- decay_log: float32 [256], P('head')
- skip_gain: float32 [256], P('head'), may hold values from 0.5 to 1.5
- entering: float32 [256, 64, 256], P('head'), may hold values from -6 to 6
- norm_gain: float32 [16384], P('head'), may hold values from 0.1 to 1.9
- w_out: bfloat16 [16384, 4096], P('head'), may hold values from -0.046875 to 0.046875
- pattern: int32 [256, 2], replicated, may hold values from 0 to 31, as said below
Outputs:
- mixed: float32 [4096, 4096], P(('ctx', 'head'))
- hessian: float32 [256, 512, 512], P(('ctx', 'head'))
The draws below stay inside these ranges and needn't reach their ends.
Inputs may be any that keep to these rules, and one draw needn't show every extreme that they name: `pattern`: all rows differ; every pair (i, i) appears, then pairs (i, i + 1) as far as they fit in 256 rows, the other rows are further pairs drawn at random; rows in random order.
All inputs are finite; a program needn't handle non-finite values.
Results may differ from the reference program's by a relative error of at most 0.0029.
Values may be sent and summed in bfloat16 or wider, within the bound.
No kernel may reach another device: no remote copies, remote signals or barrier semaphores. Data moves between devices by JAX's collectives and lax.ppermute only.
A program may use at most 128 MiB of HBM per device.

```python
import math
import jax
import jax.numpy as jnp
from jax import lax

MIXER_HEADS = 256
P_SIZE = 64
N = 256
G = 8
DOUT = 4096
BLK = 512
Q = 128
LARGE_STEP_SPOTS = 3
WINDOW_TOKENS = 4096
BLOCKS = 32
TILES = 256
NORM_GROUPS = 16


def draw_step_size(key, part):
    key = jax.random.fold_in(key, 11)
    first_key, second_random_key, third_random_key = jax.random.split(key, 3)
    base_offset = jnp.exp(jax.random.uniform(first_key, (WINDOW_TOKENS, MIXER_HEADS), jnp.float32, math.log(0.02), math.log(0.1)))
    spot_indices = jax.random.randint(second_random_key, (LARGE_STEP_SPOTS,), 0, WINDOW_TOKENS)
    struck_positions = jnp.any(jnp.arange(WINDOW_TOKENS)[:, None] == spot_indices[None, :], axis=1)
    large_step_spot = jax.random.uniform(third_random_key, (WINDOW_TOKENS, MIXER_HEADS), jnp.float32, 2.0, 4.0)
    return jnp.where(struck_positions[:, None], large_step_spot, base_offset)


def draw_decay_log(key, part):
    key = jax.random.fold_in(key, 23)
    first_key, second_random_key, third_random_key = jax.random.split(key, 3)
    slow_share = 0.5
    slowly = jax.random.uniform(first_key, (MIXER_HEADS,), jnp.float32) < slow_share
    fast_rate = jax.random.uniform(second_random_key, (MIXER_HEADS,), jnp.float32, 0.3, 0.7)
    slow_rate = jax.random.uniform(third_random_key, (MIXER_HEADS,), jnp.float32, 8.0, 40.0) / WINDOW_TOKENS
    return jnp.log(jnp.where(slowly, slow_rate, fast_rate))


def draw_pattern(key, part):
    key = jax.random.fold_in(key, 37)
    first_key, second_random_key = jax.random.split(key, 2)
    pairs = BLOCKS * BLOCKS
    spot_indices = jnp.arange(pairs, dtype=jnp.int32)
    row_index = spot_indices // BLOCKS
    column_index = spot_indices % BLOCKS
    klass = jnp.where(row_index == column_index, 0, jnp.where(column_index == row_index + 1, 1, 2))
    ranks = jax.random.permutation(first_key, pairs).astype(jnp.int32)
    scores = klass * pairs + ranks
    chosen = jnp.argsort(scores, stable=True)[:TILES].astype(jnp.int32)
    chosen = jax.random.permutation(second_random_key, chosen)
    return jnp.stack([chosen // BLOCKS, chosen % BLOCKS], axis=1).astype(jnp.int32)


def shard_levels(stream_key, dims, cuts, least, high):
    factor_of, own = 1.0, jax.random.fold_in(stream_key, 6)
    for dim, shards_of in cuts:
        steps = jnp.exp(jax.random.uniform(jax.random.fold_in(own, dim), (shards_of,), jnp.float32, least / len(cuts), high / len(cuts)))
        factor_of = factor_of * jnp.repeat(steps, dims[dim] // shards_of).reshape([-1 if axis == dim else 1 for axis in range(len(dims))])
    return factor_of


def noise(key, shape, scale, limit, cuts=(), kind=jnp.bfloat16):
    gain = shard_levels(key, shape, cuts, -0.22, 0.18) if cuts else 1.0
    array = jax.random.normal(key, shape, jnp.float32) * scale * gain
    return jnp.minimum(jnp.maximum(array, -limit), limit).astype(kind)


def setup_inputs(seed: int = 0) -> dict:
    key_list = jax.random.split(jax.random.key(seed), 12)
    return {
        "mixer_in": noise(key_list[0], (WINDOW_TOKENS, MIXER_HEADS * P_SIZE), 1.0, 6.0, ((0, 16), (1, 16))),
        "gate_in": noise(key_list[1], (WINDOW_TOKENS, MIXER_HEADS * P_SIZE), 1.0, 6.0, ((0, 16), (1, 16))),
        "b_proj": noise(key_list[2], (WINDOW_TOKENS, G * N), 1.0, 6.0, ((0, 16),)),
        "c_proj": noise(key_list[3], (WINDOW_TOKENS, G * N), N ** -0.5, 0.375, ((0, 16),)),
        "step_size": draw_step_size(jax.random.fold_in(key_list[11], 71), 0),
        "decay_log": draw_decay_log(jax.random.fold_in(key_list[11], 71), 0),
        "skip_gain": jnp.clip(0.5 + 1.0 * jax.random.uniform(key_list[6], (MIXER_HEADS,), jnp.float32) ** shard_levels(key_list[6], (MIXER_HEADS,), ((0, 16),), -0.2, 0.2), 0.5, 1.5),
        "entering": noise(key_list[7], (MIXER_HEADS, P_SIZE, N), 1.0, 6.0, ((0, 16),), jnp.float32),
        "norm_gain": jnp.clip(1.0 + 0.18 * jax.random.normal(key_list[8], (MIXER_HEADS * P_SIZE,), jnp.float32), 0.1, 1.9),
        "w_out": noise(key_list[9], (MIXER_HEADS * P_SIZE, DOUT), (MIXER_HEADS * P_SIZE) ** -0.5, 0.046875, ((0, 16),)),
        "pattern": draw_pattern(jax.random.fold_in(key_list[11], 71), 0),
    }


EPS = 1e-05
HIGHEST_PRECISION = lax.Precision.HIGHEST

def reference(mixer_in, gate_in, b_proj, c_proj, step_size, decay_log, skip_gain, entering, norm_gain, w_out, pattern):
    stretch_count = WINDOW_TOKENS // Q
    rates = -jnp.exp(decay_log)
    log_decay = step_size * rates[None, :]
    inputs_wide = mixer_in.astype(jnp.float32).reshape(WINDOW_TOKENS, MIXER_HEADS, P_SIZE)
    head_group = (jnp.arange(MIXER_HEADS) // (MIXER_HEADS // G)).astype(jnp.int32)
    lower_mask = jnp.tril(jnp.ones((Q, Q), dtype=bool))

    def advance(carried, stretch_item):
        inputs_block, b_block, c_block, log_block, step_block = stretch_item
        b_heads = b_block[:, head_group, :]
        c_heads = c_block[:, head_group, :]
        cumul = jnp.cumsum(log_block, axis=0)
        cumul_turned = cumul.T
        differ = cumul_turned[:, :, None] - cumul_turned[:, None, :]
        lower_decay = jnp.where(lower_mask[None], jnp.exp(jnp.where(lower_mask[None], differ, 0.0)), 0.0)
        scores = jnp.einsum('thn,shn->hts', c_heads, b_heads, precision=HIGHEST_PRECISION)
        weighted = step_block[:, :, None] * inputs_block
        outputs = jnp.einsum('hts,shp->thp', lower_decay * scores, weighted, precision=HIGHEST_PRECISION)
        outputs = outputs + jnp.exp(cumul)[:, :, None] * jnp.einsum('thn,hpn->thp', c_heads, carried, precision=HIGHEST_PRECISION)
        end_weight = jnp.exp(cumul[-1][None, :] - cumul)
        updated = jnp.exp(cumul[-1])[:, None, None] * carried + jnp.einsum('sh,shp,shn->hpn', end_weight, weighted, b_heads, precision=HIGHEST_PRECISION)
        return (updated, outputs)
    b_wide = b_proj.astype(jnp.float32).reshape(stretch_count, Q, G, N)
    c_wide = c_proj.astype(jnp.float32).reshape(stretch_count, Q, G, N)
    items = (inputs_wide.reshape(stretch_count, Q, MIXER_HEADS, P_SIZE), b_wide, c_wide, log_decay.reshape(stretch_count, Q, MIXER_HEADS), step_size.reshape(stretch_count, Q, MIXER_HEADS))
    final_state, stretch_out = lax.scan(advance, entering.astype(jnp.float32), items)
    mixer_out = stretch_out.reshape(WINDOW_TOKENS, MIXER_HEADS, P_SIZE) + skip_gain[None, :, None] * inputs_wide
    gated = mixer_out.reshape(WINDOW_TOKENS, MIXER_HEADS * P_SIZE) * jax.nn.silu(gate_in.astype(jnp.float32))
    grouped = gated.reshape(WINDOW_TOKENS, NORM_GROUPS, MIXER_HEADS * P_SIZE // NORM_GROUPS)
    normed = grouped * lax.rsqrt(lax.optimization_barrier(jnp.mean(grouped * grouped, axis=-1, keepdims=True)) + EPS)
    features = (normed.reshape(WINDOW_TOKENS, MIXER_HEADS * P_SIZE) * norm_gain[None, :]).astype(jnp.bfloat16)
    mixed = jnp.dot(features, w_out, preferred_element_type=jnp.float32)
    blocks = features.reshape(WINDOW_TOKENS, BLOCKS, BLK)
    factor = 2.0 / WINDOW_TOKENS

    def one_tile(pair_row):
        row_block = lax.dynamic_index_in_dim(blocks, pair_row[0], 1, keepdims=False)
        column_block = lax.dynamic_index_in_dim(blocks, pair_row[1], 1, keepdims=False)
        return jnp.dot(row_block.T, column_block, preferred_element_type=jnp.float32) * factor
    hessian = lax.map(one_tile, pattern)
    return (mixed, hessian)
```

```python
import functools

import jax
import jax.numpy as jnp
from jax import lax
from jax.experimental import pallas as pl
from jax.experimental.pallas import tpu as pltpu
from jax.sharding import Mesh, PartitionSpec as P

G = 8
N = 256
BLK = 512
HEADS = 16
PS = 64
TOK = 256
COLS = HEADS * PS
CTXN = 16
EPS = 1e-05
F32, BF16, F16 = jnp.float32, jnp.bfloat16, jnp.float16
HI = lax.Precision.HIGHEST
XB_MAX = 36.0
ENTER_MAX = 8.0
TINY = 1e-30
TOP = 14.0
LAST = 1000.0
PAY = HEADS // 2 * 16 + 8
TILE_SCALE = 2.0**-8

CTX = ("x_hi", "z")
HEAD = ("y", "x_lo", "core")
ROWS0 = (((0,), (0,)), ((), ()))
ROWS1 = (((1,), (1,)), ((), ()))


def two(v):
    hi = v.astype(BF16)
    return hi, (v - hi.astype(F32)).astype(BF16)


def pair(w, j, lanes):
    return jnp.where(lanes < PS, w[:, 2 * j : 2 * j + 1], w[:, 2 * j + 1 : 2 * j + 2])


def exponent(bound):
    return jnp.clip(jnp.ceil(jnp.log2(jnp.maximum(bound, TINY))) + 1.0, -100.0, 127.0)


def start_kernel(g_ref, x_ref, b_ref, step_ref, dlog_ref, pay_ref, cum_ref, cumt_ref, stept_ref, hi_ref, lo_ref, extra_ref):
    step = step_ref[...]
    logd = step * (-jnp.exp(dlog_ref[...]))
    row = lax.broadcasted_iota(jnp.int32, (TOK, TOK), 0)
    col = lax.broadcasted_iota(jnp.int32, (TOK, TOK), 1)
    cum = jnp.dot((row >= col).astype(F32), logd, precision=HI, preferred_element_type=F32)
    cum_ref[...] = cum
    cumt_ref[...] = lax.dot_general(logd, (row <= col).astype(F32), ROWS0, precision=HI, preferred_element_type=F32)
    stept_ref[...] = lax.dot_general(step, (row == col).astype(F32), ROWS0, precision=HI, preferred_element_type=F32)
    total = cum[TOK - 1 : TOK, :]
    w = step * jnp.exp(total - cum)
    e = exponent(XB_MAX * jnp.sum(jnp.abs(w), axis=0, keepdims=True))
    total = jnp.clip(total, -LAST, LAST)
    t0 = total.astype(BF16).astype(F32)
    t1 = (total - t0).astype(BF16).astype(F32)
    extra_ref[...] = jnp.zeros((8, 128), F32)
    for i, v in enumerate((t0, t1, total - t0 - t1, e)):
        extra_ref[i : i + 1, :HEADS] = v
    extra = extra_ref[...]
    w = w * jnp.exp2(TOP - e)
    lanes = lax.broadcasted_iota(jnp.int32, (TOK, 128), 1)
    for j in range(HEADS // 2):
        cols = slice(128 * j, 128 * j + 128)
        hi, lo = two(pair(w, j, lanes) * x_ref[:, cols].astype(F32))
        hi_ref[:, cols] = hi
        lo_ref[:, cols] = lo
    b = b_ref[...]
    state = lax.dot_general(b, hi_ref[...], ROWS0, preferred_element_type=F32) + lax.dot_general(
        b, lo_ref[...], ROWS0, preferred_element_type=F32
    )
    for c in range(CTXN):
        for j in range(HEADS // 2):
            pay_ref[c, 16 * j : 16 * j + 16, :] = state[16 * c : 16 * c + 16, 128 * j : 128 * j + 128]
        pay_ref[c, PAY - 8 :, :] = extra


def scan_kernel(at_ref, q_ref, enter_ref, out_ref):
    head = lax.broadcasted_iota(jnp.int32, (128, COLS), 0)
    spread = (lax.broadcasted_iota(jnp.int32, (128, COLS), 1) // PS == head).astype(F32)

    def wide(v):
        return jnp.dot(v, spread, precision=HI, preferred_element_type=F32)

    info = [jnp.concatenate([q_ref[c, PAY - 8 + i : PAY - 7 + i, :] for c in range(CTXN)], axis=0) for i in range(4)]
    d = jnp.exp(info[0] + info[1] + info[2])
    w = jnp.exp2(info[3])
    bounds = [jnp.full((1, 128), ENTER_MAX, F32)]
    for c in range(CTXN - 1):
        bounds.append(d[c : c + 1] * bounds[-1] + w[c : c + 1])
    e = exponent(jnp.concatenate(bounds, axis=0))
    dw, qw, ow = wide(d), wide(jnp.exp2(info[3] - TOP)), wide(jnp.exp2(TOP - e))
    rows = N // CTXN
    mine = lax.broadcasted_iota(jnp.int32, (rows, N), 0) + at_ref[1] * rows
    pick = (lax.broadcasted_iota(jnp.int32, (rows, N), 1) == mine).astype(F32)
    s = lax.dot_general(pick, enter_ref[...], ROWS1, precision=HI, preferred_element_type=F32)
    for j in range(HEADS // 2):
        cols = slice(128 * j, 128 * j + 128)
        here = slice(16 * j, 16 * j + 16)
        sj = s[:, cols]
        for c in range(CTXN):
            out_ref[c, here, :] = sj * ow[c : c + 1, cols]
            sj = dw[c : c + 1, cols] * sj + q_ref[c, here, :] * qw[c : c + 1, cols]
    for c in range(CTXN):
        out_ref[c, PAY - 8 :, :] = jnp.broadcast_to(e[c : c + 1], (8, 128))


def finish_kernel(
    g_ref, x_ref, gate_ref, b_ref, c_ref, cum_ref, cumt_ref, stept_ref, skip_ref, gain_ref, in_ref,
    out_ref, a_ref, b2_ref, gated_ref
):
    c = c_ref[...]
    b = b_ref[...]
    scores = lax.dot_general(c, b, ROWS1, preferred_element_type=F32)
    cum = cum_ref[...]
    carry = jnp.exp(cum) * jnp.exp2(in_ref[0, PAY - 8 : PAY - 7, :HEADS] - TOP)
    skip = skip_ref[...]
    half = TOK // 2
    total = jnp.zeros((TOK, 1), F32)
    lanes = lax.broadcasted_iota(jnp.int32, (TOK, 128), 1)
    lane_half = lax.broadcasted_iota(jnp.int32, (half, 128), 1)
    for j in range(HEADS // 2):
        cols = slice(128 * j, 128 * j + 128)
        x = x_ref[:, cols]
        hi, lo = two(in_ref[:, 16 * j : 16 * j + 16, :].reshape(N, 128))
        inbound = jnp.dot(c, hi, preferred_element_type=F32) + jnp.dot(c, lo, preferred_element_type=F32)
        parts = []
        for r0, r1 in ((0, half), (half, TOK)):
            row = lax.broadcasted_iota(jnp.int32, (half, r1), 0) + r0
            col = lax.broadcasted_iota(jnp.int32, (half, r1), 1)
            mask = row >= col
            outs = []
            for h in (2 * j, 2 * j + 1):
                differ = cum[r0:r1, h : h + 1] - cumt_ref[h : h + 1, :r1]
                decay = jnp.where(mask, jnp.exp(jnp.where(mask, differ, 0.0)), 0.0)
                hi, lo = two(decay * scores[r0:r1, :r1] * stept_ref[h : h + 1, :r1])
                outs.append(
                    jnp.dot(hi, x[:r1], preferred_element_type=F32) + jnp.dot(lo, x[:r1], preferred_element_type=F32)
                )
            parts.append(jnp.where(lane_half < PS, outs[0], outs[1]))
        y = jnp.concatenate(parts, axis=0)
        y = y + inbound * pair(carry, j, lanes) + pair(skip, j, lanes[:1]) * x.astype(F32)
        g = gate_ref[:, cols].astype(F32)
        gated = y * (g / (1.0 + jnp.exp(-g)))
        gated_ref[:, cols] = gated
        total = total + jnp.sum(gated * gated, axis=1, keepdims=True)
    scale = lax.rsqrt(total / COLS + EPS)
    features = (gated_ref[...] * scale * gain_ref[...]).astype(BF16)
    out_ref[...] = features
    a_ref[0] = features[:half]
    b2_ref[0] = features[half:]


def tile_kernel(where_ref, *refs):
    sources, out_ref, held, sems = (refs[:10], refs[10:20]), refs[20], refs[21], refs[22]
    k, count = pl.program_id(0), pl.num_programs(0)
    places = [(o, x, half) for o in range(2) for x in range(2) for half in range(2)]

    def copy(source, spot, column, slot, place):
        return pltpu.make_async_copy(
            source.at[spot, :, pl.ds(column, BLK)], held.at[(slot,) + place], sems.at[(slot,) + place]
        )

    def fetch(tile, slot):
        for n, place in enumerate(places):
            base = (tile * 8 + n) * 3
            which, spot = where_ref[base], where_ref[base + 1]
            column = pl.multiple_of(where_ref[base + 2] * BLK, BLK)
            for i in range(10):
                @pl.when(which == i)
                def _():
                    copy(sources[place[2]][i], spot, column, slot, place).start()

    @pl.when(k == 0)
    def _():
        fetch(0, 0)

    @pl.when(k + 1 < count)
    def _():
        fetch(k + 1, (k + 1) % 2)

    slot = k % 2
    for place in places:
        copy(sources[0][0], 0, 0, slot, place).wait()
    a = held[slot, 0].reshape(BLK, BLK)
    b = held[slot, 1].reshape(BLK, BLK)
    out_ref[0] = lax.dot_general(a, b, ROWS0, preferred_element_type=F32) * TILE_SCALE


def whole(shape):
    return pl.BlockSpec(shape, lambda *_: (0,) * len(shape))


def moved(v, axis, by):
    n = lax.axis_size(axis)
    return lax.ppermute(v, axis, [(i, (i - by) % n) for i in range(n)])


def spread_plane(v, first, second):
    n = v.shape[1] // 2
    plus, minus = moved(v, first, 1), moved(v, first, -1)
    far = jnp.concatenate([moved(plus[:, :n], first, 1), moved(minus[:, n:], first, -1)], axis=1)
    line = jnp.concatenate([v, plus, minus, far], axis=0)
    plus, minus = moved(line, second, 1), moved(line, second, -1)
    own = [line, plus, minus, moved(plus[:2], second, 1), moved(minus[2:], second, -1)]
    return own + [moved(w, "core", 1) for w in own]


def place_of(d):
    d = d % 4
    return jnp.where(d == 2, 3, jnp.where(d == 3, 2, d))


def where_found(blocks):
    head = blocks[:, :, None] // 2
    x = 2 * jnp.arange(2)[None, None, :] + head // 2 % 2
    x = place_of(x - lax.axis_index(("x_hi", "x_lo")))
    y = place_of(head // 4 - lax.axis_index("y")) + 0 * x
    other = (head % 2 != lax.axis_index("core")) * 5 + 0 * x
    column = blocks[:, :, None] % 2 + 0 * x

    def found(outer, inner):
        last = (outer == 3) & (inner >= 2)
        return jnp.stack([outer + last + other, inner - 2 * last, column], axis=-1)

    return jnp.stack([found(y, x), found(x, y)], axis=3).astype(jnp.int32).reshape(-1)


def make_tiles(where, arrays, count):
    return pl.pallas_call(
        tile_kernel,
        grid_spec=pltpu.PrefetchScalarGridSpec(
            num_scalar_prefetch=1,
            grid=(count,),
            in_specs=[pl.BlockSpec(memory_space=pl.ANY)] * 20,
            out_specs=pl.BlockSpec((1, BLK, BLK), lambda k, w: (k, 0, 0)),
            scratch_shapes=[
                pltpu.VMEM((2, 2, 2, 2, TOK // 2, BLK), BF16), pltpu.SemaphoreType.DMA((2, 2, 2, 2))
            ],
        ),
        out_shape=jax.ShapeDtypeStruct((count, BLK, BLK), F32),
        compiler_params=pltpu.CompilerParams(vmem_limit_bytes=32 * 1024 * 1024),
        cost_estimate=pl.CostEstimate(
            flops=count * 2 * BLK**3, bytes_accessed=count * 2 * 1024 * 1024, transcendentals=0
        ),
        name="hessian_tiles",
    )(where, *arrays)


def sum_over_z(order, tiles):
    n = BLK // 2
    four = tiles(4).astype(F16)
    up, down = moved(four[:n], "z", -1), moved(four[n:], "z", 1)
    up, down = (
        jnp.concatenate([up.astype(F32) + tiles(3)[:n], tiles(3)[n:]], axis=0).astype(F16),
        jnp.concatenate([tiles(5)[:n], down.astype(F32) + tiles(5)[n:]], axis=0).astype(F16),
    )
    for r in (2, 1):
        up, down = moved(up, "z", -1), moved(down, "z", 1)
        up = (up.astype(F32) + tiles(r)).astype(F16)
        down = (down.astype(F32) + tiles(8 - r)).astype(F16)
    up, down = moved(up, "z", -1), moved(down, "z", 1)
    return (tiles(0) + up.astype(F32) + down.astype(F32)) * (2.0 / 4096 / TILE_SCALE)


def body(
    mixer_in, gate_in, b_proj, c_proj, step_size, decay_log, skip_gain, entering, norm_gain, w_out, pattern
):
    ctx_at = lax.axis_index(CTX)
    head_at = lax.axis_index(HEAD)
    place = jnp.stack([head_at * HEADS // (256 // G), ctx_at]).astype(jnp.int32)
    group = pl.BlockSpec((TOK, N), lambda i, g: (0, g[0]))
    params = pltpu.CompilerParams(vmem_limit_bytes=48 * 1024 * 1024)
    sds = jax.ShapeDtypeStruct

    sent, cum, cumt, stept = pl.pallas_call(
        start_kernel,
        grid_spec=pltpu.PrefetchScalarGridSpec(
            num_scalar_prefetch=1,
            grid=(1,),
            in_specs=[whole((TOK, COLS)), group, whole((TOK, HEADS)), whole((1, HEADS))],
            out_specs=[whole((CTXN, PAY, 128)), whole((TOK, HEADS)), whole((HEADS, TOK)), whole((HEADS, TOK))],
            scratch_shapes=[pltpu.VMEM((TOK, COLS), BF16)] * 2 + [pltpu.VMEM((8, 128), F32)],
        ),
        out_shape=[
            sds((CTXN, PAY, 128), F32), sds((TOK, HEADS), F32), sds((HEADS, TOK), F32), sds((HEADS, TOK), F32)
        ],
        compiler_params=params,
        name="mixer_start",
    )(place, mixer_in, b_proj, step_size, decay_log[None, :])

    sent = lax.all_to_all(sent.astype(F16), CTX, 0, 0, tiled=True).astype(F32)
    incoming = pl.pallas_call(
        scan_kernel,
        grid_spec=pltpu.PrefetchScalarGridSpec(
            num_scalar_prefetch=1,
            grid=(1,),
            in_specs=[whole((CTXN, PAY, 128)), whole((COLS, N))],
            out_specs=whole((CTXN, PAY, 128)),
        ),
        out_shape=sds((CTXN, PAY, 128), F32),
        compiler_params=params,
        name="state_scan",
    )(place, sent, entering.reshape(COLS, N))
    incoming = lax.all_to_all(incoming.astype(F16), CTX, 0, 0, tiled=True).astype(F32)

    half = whole((1, TOK // 2, COLS))
    features, first, second = pl.pallas_call(
        finish_kernel,
        grid_spec=pltpu.PrefetchScalarGridSpec(
            num_scalar_prefetch=1,
            grid=(1,),
            in_specs=[
                whole((TOK, COLS)), whole((TOK, COLS)), group, group, whole((TOK, HEADS)), whole((HEADS, TOK)),
                whole((HEADS, TOK)), whole((1, HEADS)), whole((1, COLS)), whole((CTXN, PAY, 128)),
            ],
            out_specs=[whole((TOK, COLS)), half, half],
            scratch_shapes=[pltpu.VMEM((TOK, COLS), F32)],
        ),
        out_shape=[sds((TOK, COLS), BF16)] + [sds((1, TOK // 2, COLS), BF16)] * 2,
        compiler_params=params,
        name="mixer_finish",
    )(place, mixer_in, gate_in, b_proj, c_proj, cum, cumt, stept, skip_gain[None, :], norm_gain[None, :], incoming)

    X, Y = ("x_hi", "x_lo"), "y"
    arrays = spread_plane(first, X, Y) + spread_plane(second, Y, X)
    mixed = lax.psum_scatter(
        jnp.dot(features, w_out, preferred_element_type=F32), HEAD, scatter_dimension=0, tiled=True
    )
    owned = pattern.reshape(2, 8, 16, 2)[lax.axis_index("x_hi"), :, head_at]
    order = (4, 3, 5, 2, 6, 1, 7, 0)
    where = where_found(owned[(lax.axis_index("z") + jnp.array(order)) % 8])
    per = where.shape[0] // 8
    one = make_tiles(where[:per], arrays, 1)
    rest = make_tiles(where[per:], arrays, 7)
    hessian = sum_over_z(order, lambda r: one[0] if r == 4 else rest[order.index(r) - 1])
    return mixed, hessian[None]


def solution(mesh):
    fine = Mesh(mesh.devices.reshape(2, 8, 4, 2, 2), CTX + HEAD)
    in_specs = (
        P(CTX, HEAD), P(CTX, HEAD), P(CTX, None), P(CTX, None), P(CTX, HEAD), P(HEAD), P(HEAD),
        P(HEAD, None, None), P(HEAD), P(HEAD, None), P(),
    )
    out_specs = (P(CTX + HEAD, None), P(CTX + HEAD, None, None))
    return jax.shard_map(body, mesh=fine, in_specs=in_specs, out_specs=out_specs, check_vma=False)
```

```python
import functools

import jax
import jax.numpy as jnp
from jax import lax
from jax.experimental import pallas as pl
from jax.experimental.pallas import tpu as pltpu
from jax.sharding import Mesh, PartitionSpec as P

G = 8
N = 256
BLK = 512
HEADS = 16
PS = 64
TOK = 256
COLS = HEADS * PS
CTXN = 16
EPS = 1e-05
F32, BF16, F16 = jnp.float32, jnp.bfloat16, jnp.float16
HI = lax.Precision.HIGHEST
XB_MAX = 36.0
ENTER_MAX = 8.0
TINY = 1e-30
TOP = 14.0
LAST = 1000.0
PAY = HEADS // 2 * 16 + 8
ORDER = (4, 3, 5, 2, 6, 1, 7, 0)
VMEM = 24 * 1024 * 1024
SOURCES = 10
TILE_SCALE = 2.0**-8

CTX = ("x_hi", "z")
HEAD = ("y", "x_lo", "core")
ROWS0 = (((0,), (0,)), ((), ()))
ROWS1 = (((1,), (1,)), ((), ()))


def two(v):
    hi = v.astype(BF16)
    return hi, (v - hi.astype(F32)).astype(BF16)


def pair(w, j, lanes):
    return jnp.where(lanes < PS, w[:, 2 * j : 2 * j + 1], w[:, 2 * j + 1 : 2 * j + 2])


def exponent(bound):
    return jnp.clip(jnp.ceil(jnp.log2(jnp.maximum(bound, TINY))) + 1.0, -100.0, 127.0)


def start_kernel(g_ref, x_ref, b_ref, stept_ref, dlog_ref, pay_ref, cum_ref, cumt_ref, hi_ref, lo_ref, extra_ref):
    stept = stept_ref[...]
    own = lax.broadcasted_iota(jnp.int32, (HEADS, HEADS), 0) == lax.broadcasted_iota(jnp.int32, (HEADS, HEADS), 1)
    rate = -jnp.sum(jnp.where(own, jnp.exp(dlog_ref[...]), 0.0), axis=1, keepdims=True)
    logdt = stept * rate
    row = lax.broadcasted_iota(jnp.int32, (TOK, TOK), 0)
    col = lax.broadcasted_iota(jnp.int32, (TOK, TOK), 1)
    cum = lax.dot_general((row >= col).astype(F32), logdt, ROWS1, precision=HI, preferred_element_type=F32)
    cum_ref[...] = cum
    cumt_ref[...] = jnp.dot(logdt, (row <= col).astype(F32), precision=HI, preferred_element_type=F32)
    step = lax.dot_general((row == col).astype(F32), stept, ROWS1, precision=HI, preferred_element_type=F32)
    total = cum[TOK - 1 : TOK, :]
    w = step * jnp.exp(total - cum)
    e = exponent(XB_MAX * jnp.sum(jnp.abs(w), axis=0, keepdims=True))
    total = jnp.clip(total, -LAST, LAST)
    t0 = total.astype(BF16).astype(F32)
    t1 = (total - t0).astype(BF16).astype(F32)
    extra_ref[...] = jnp.zeros((8, 128), F32)
    for i, v in enumerate((t0, t1, total - t0 - t1, e)):
        extra_ref[i : i + 1, :HEADS] = v
    extra = extra_ref[...]
    w = w * jnp.exp2(TOP - e)
    lanes = lax.broadcasted_iota(jnp.int32, (TOK, 128), 1)
    for j in range(HEADS // 2):
        cols = slice(128 * j, 128 * j + 128)
        hi, lo = two(pair(w, j, lanes) * x_ref[:, cols].astype(F32))
        hi_ref[:, cols] = hi
        lo_ref[:, cols] = lo
    b = b_ref[...]
    state = lax.dot_general(b, hi_ref[...], ROWS0, preferred_element_type=F32) + lax.dot_general(
        b, lo_ref[...], ROWS0, preferred_element_type=F32
    )
    for c in range(CTXN):
        for j in range(HEADS // 2):
            pay_ref[c, 16 * j : 16 * j + 16, :] = state[16 * c : 16 * c + 16, 128 * j : 128 * j + 128]
        pay_ref[c, PAY - 8 :, :] = extra


def scan_kernel(at_ref, q_ref, enter_ref, out_ref):
    head = lax.broadcasted_iota(jnp.int32, (128, COLS), 0)
    spread = (lax.broadcasted_iota(jnp.int32, (128, COLS), 1) // PS == head).astype(F32)

    def wide(v):
        return jnp.dot(v, spread, precision=HI, preferred_element_type=F32)

    info = [jnp.concatenate([q_ref[c, PAY - 8 + i : PAY - 7 + i, :] for c in range(CTXN)], axis=0) for i in range(4)]
    d = jnp.exp(info[0] + info[1] + info[2])
    w = jnp.exp2(info[3])
    bounds = [jnp.full((1, 128), ENTER_MAX, F32)]
    for c in range(CTXN - 1):
        bounds.append(d[c : c + 1] * bounds[-1] + w[c : c + 1])
    e = exponent(jnp.concatenate(bounds, axis=0))
    dw, qw, ow = wide(d), wide(jnp.exp2(info[3] - TOP)), wide(jnp.exp2(TOP - e))
    rows = N // CTXN
    mine = lax.broadcasted_iota(jnp.int32, (rows, N), 0) + at_ref[1] * rows
    pick = (lax.broadcasted_iota(jnp.int32, (rows, N), 1) == mine).astype(F32)
    s = lax.dot_general(pick, enter_ref[...], ROWS1, precision=HI, preferred_element_type=F32)
    for j in range(HEADS // 2):
        cols = slice(128 * j, 128 * j + 128)
        here = slice(16 * j, 16 * j + 16)
        sj = s[:, cols]
        for c in range(CTXN):
            out_ref[c, here, :] = sj * ow[c : c + 1, cols]
            sj = dw[c : c + 1, cols] * sj + q_ref[c, here, :] * qw[c : c + 1, cols]
    for c in range(CTXN):
        out_ref[c, PAY - 8 :, :] = jnp.broadcast_to(e[c : c + 1], (8, 128))


def inner_kernel(g_ref, x_ref, b_ref, c_ref, cum_ref, cumt_ref, stept_ref, skip_ref, out_ref):
    scores = lax.dot_general(c_ref[...], b_ref[...], ROWS1, preferred_element_type=F32)
    cum = cum_ref[...]
    skip = skip_ref[...]
    half = TOK // 2
    lanes = lax.broadcasted_iota(jnp.int32, (half, 128), 1)
    for j in range(HEADS // 2):
        cols = slice(128 * j, 128 * j + 128)
        x = x_ref[:, cols]
        for r0, r1 in ((0, half), (half, TOK)):
            row = lax.broadcasted_iota(jnp.int32, (half, r1), 0) + r0
            col = lax.broadcasted_iota(jnp.int32, (half, r1), 1)
            mask = row >= col
            outs = []
            for h in (2 * j, 2 * j + 1):
                differ = cum[r0:r1, h : h + 1] - cumt_ref[h : h + 1, :r1]
                decay = jnp.where(mask, jnp.exp(jnp.where(mask, differ, 0.0)), 0.0)
                hi, lo = two(decay * scores[r0:r1, :r1] * stept_ref[h : h + 1, :r1])
                outs.append(
                    jnp.dot(hi, x[:r1], preferred_element_type=F32) + jnp.dot(lo, x[:r1], preferred_element_type=F32)
                )
            y = jnp.where(lanes < PS, outs[0], outs[1])
            out_ref[r0:r1, cols] = y + pair(skip, j, lanes[:1]) * x[r0:r1].astype(F32)


def finish_kernel(g_ref, y_ref, gate_ref, c_ref, cum_ref, gain_ref, in_ref, keep_ref, give_ref, gated_ref):
    c = c_ref[...]
    carry = jnp.exp(cum_ref[...]) * jnp.exp2(in_ref[0, PAY - 8 : PAY - 7, :HEADS] - TOP)
    half = TOK // 2
    total = jnp.zeros((TOK, 1), F32)
    lanes = lax.broadcasted_iota(jnp.int32, (TOK, 128), 1)
    for j in range(HEADS // 2):
        cols = slice(128 * j, 128 * j + 128)
        hi, lo = two(in_ref[:, 16 * j : 16 * j + 16, :].reshape(N, 128))
        inbound = jnp.dot(c, hi, preferred_element_type=F32) + jnp.dot(c, lo, preferred_element_type=F32)
        y = y_ref[:, cols] + inbound * pair(carry, j, lanes)
        g = gate_ref[:, cols].astype(F32)
        gated = y * (g / (1.0 + jnp.exp(-g)))
        gated_ref[:, cols] = gated
        total = total + jnp.sum(gated * gated, axis=1, keepdims=True)
    scale = lax.rsqrt(total / COLS + EPS)
    features = (gated_ref[...] * scale * gain_ref[...]).reshape(TOK // 32, 2, 16, COLS)
    even, odd = features[:, 0].reshape(half, COLS), features[:, 1].reshape(half, COLS)
    first = g_ref[2] == 0
    keep_ref[0] = jnp.where(first, even, odd).astype(BF16)
    give_ref[0] = jnp.where(first, odd, even).astype(BF16)


def tile_kernel(counts, where_ref, *refs):
    sources, out_refs, (held, sems) = refs[:SOURCES], refs[SOURCES:-2], refs[-2:]
    k, count = pl.program_id(0), pl.num_programs(0)
    places = [(o, x) for o in range(2) for x in range(2)]

    def copy(source, spot, column, slot, place):
        return pltpu.make_async_copy(
            source.at[spot, :, pl.ds(column, BLK)], held.at[(slot,) + place], sems.at[(slot,) + place]
        )

    def start_from(low, high, which, made):
        if high - low == 1:
            made(low).start()
            return
        middle = (low + high) // 2
        pl.when(which < middle)(lambda: start_from(low, middle, which, made))
        pl.when(which >= middle)(lambda: start_from(middle, high, which, made))

    def fetch(tile, slot):
        for n, place in enumerate(places):
            base = (tile * 4 + n) * 3
            which, spot = where_ref[base], where_ref[base + 1]
            column = pl.multiple_of(where_ref[base + 2] * BLK, BLK)
            start_from(0, SOURCES, which, lambda i: copy(sources[i], spot, column, slot, place))

    @pl.when(k == 0)
    def _():
        fetch(0, 0)

    @pl.when(k + 1 < count)
    def _():
        fetch(k + 1, (k + 1) % 2)

    slot = k % 2
    for place in places:
        copy(sources[0], 0, 0, slot, place).wait()
    a = held[slot, 0].reshape(TOK, BLK)
    b = held[slot, 1].reshape(TOK, BLK)
    tile = lax.dot_general(a, b, ROWS0, preferred_element_type=F32) * TILE_SCALE

    at = 0
    for ref, n in zip(out_refs, counts):

        @pl.when((k >= at) & (k < at + n))
        def _(ref=ref):
            ref[0] = tile

        at += n


def whole(shape):
    return pl.BlockSpec(shape, lambda *_: (0,) * len(shape))


def moved(v, axis, by):
    n = lax.axis_size(axis)
    return lax.ppermute(v, axis, [(i, (i - by) % n) for i in range(n)])


def around(v, axis):
    return [v, moved(v, axis, 1), moved(v, axis, -1), moved(v, axis, 2)]


def copy_kernel(count, pieces, *refs):
    for a, low, n, o, to in pieces:
        refs[count + o][to : to + n] = refs[a][low : low + n]


def copied(arrays, sizes, pieces):
    shape, dtype = arrays[0].shape[1:], arrays[0].dtype
    return pl.pallas_call(
        functools.partial(copy_kernel, len(arrays), pieces),
        out_shape=[jax.ShapeDtypeStruct((n,) + shape, dtype) for n in sizes],
        compiler_params=pltpu.CompilerParams(vmem_limit_bytes=VMEM),
        cost_estimate=pl.CostEstimate(flops=0, bytes_accessed=2 * sum(sizes) * 2**18, transcendentals=0),
        name="pieces",
    )(*arrays)


def across(line, axis):
    plus, minus = moved(line, axis, 1), moved(line, axis, -1)
    near, rest = copied([plus, minus], (2, 2), ((0, 0, 2, 0, 0), (1, 2, 2, 1, 0)))
    return [line, plus, minus, moved(near, axis, 1), moved(rest, axis, -1)]


def place_of(d):
    d = d % 4
    return jnp.where(d == 2, 3, jnp.where(d == 3, 2, d))


def where_found(blocks):
    head = blocks[:, :, None] // 2
    x = 2 * jnp.arange(2)[None, None, :] + head // 2 % 2
    x = place_of(x - lax.axis_index(("x_hi", "x_lo")))
    y = place_of(head // 4 - lax.axis_index("y")) + 0 * x
    other = (head % 2 != lax.axis_index("core")) + 0 * x
    outer, inner = jnp.where(other == 1, x, y), jnp.where(other == 1, y, x)
    last = (outer == 3) & (inner >= 2)
    found = (outer + last + other * 5, inner - 2 * last, blocks[:, :, None] % 2 + 0 * x)
    return jnp.stack(found, axis=-1).astype(jnp.int32).reshape(blocks.shape[0], 12)


def make_tiles(where, arrays, counts, kept):
    count, at, specs = sum(counts), 0, []
    for n in counts:
        specs.append(pl.BlockSpec((1, BLK, BLK), lambda k, w, at=at, n=n: (jnp.clip(k - at, 0, n - 1), 0, 0)))
        at += n
    return pl.pallas_call(
        functools.partial(tile_kernel, counts),
        grid_spec=pltpu.PrefetchScalarGridSpec(
            num_scalar_prefetch=1,
            grid=(count,),
            in_specs=[pl.BlockSpec(memory_space=pl.ANY)] * SOURCES,
            out_specs=specs,
            scratch_shapes=[pltpu.VMEM((2, 2, 2, TOK // 2, BLK), BF16), pltpu.SemaphoreType.DMA((2, 2, 2))],
        ),
        out_shape=[(jax.ShapeDtypeStruct if n in kept else pltpu.HBM)((counts[n], BLK, BLK), F32) for n in range(len(counts))],
        compiler_params=pltpu.CompilerParams(vmem_limit_bytes=VMEM),
        cost_estimate=pl.CostEstimate(
            flops=count * BLK**3, bytes_accessed=count * 2 * 1024 * 1024, transcendentals=0
        ),
        name="hessian_tiles",
    )(where.reshape(-1), *arrays)


def body(
    mixer_in, gate_in, b_proj, c_proj, step_size, decay_log, skip_gain, entering, norm_gain, w_out, pattern
):
    ctx_at = lax.axis_index(CTX)
    head_at = lax.axis_index(HEAD)
    place = jnp.stack([head_at * HEADS // (256 // G), ctx_at, lax.axis_index("core")]).astype(jnp.int32)
    group = pl.BlockSpec((TOK, N), lambda i, g: (0, g[0]))
    params = pltpu.CompilerParams(vmem_limit_bytes=VMEM)
    sds = jax.ShapeDtypeStruct

    stept = step_size.T
    sent, cum, cumt = pl.pallas_call(
        start_kernel,
        grid_spec=pltpu.PrefetchScalarGridSpec(
            num_scalar_prefetch=1,
            grid=(1,),
            in_specs=[whole((TOK, COLS)), group, whole((HEADS, TOK)), whole((1, HEADS))],
            out_specs=[whole((CTXN, PAY, 128)), whole((TOK, HEADS)), whole((HEADS, TOK))],
            scratch_shapes=[pltpu.VMEM((TOK, COLS), BF16)] * 2 + [pltpu.VMEM((8, 128), F32)],
        ),
        out_shape=[sds((CTXN, PAY, 128), F32), sds((TOK, HEADS), F32), sds((HEADS, TOK), F32)],
        compiler_params=params,
        name="mixer_start",
    )(place, mixer_in, b_proj, stept, decay_log[None, :])

    w_other = moved(w_out, "core", 1)
    sent = lax.all_to_all(sent.astype(F16), CTX, 0, 0, tiled=True)
    sent, w_other = lax.optimization_barrier((sent, w_other))
    sent = sent.astype(F32)
    incoming = pl.pallas_call(
        scan_kernel,
        grid_spec=pltpu.PrefetchScalarGridSpec(
            num_scalar_prefetch=1,
            grid=(1,),
            in_specs=[whole((CTXN, PAY, 128)), whole((COLS, N))],
            out_specs=whole((CTXN, PAY, 128)),
        ),
        out_shape=sds((CTXN, PAY, 128), F32),
        compiler_params=params,
        name="state_scan",
    )(place, sent, entering.reshape(COLS, N))
    incoming = lax.all_to_all(incoming.astype(F16), CTX, 0, 0, tiled=True).astype(F32)

    inner = pl.pallas_call(
        inner_kernel,
        grid_spec=pltpu.PrefetchScalarGridSpec(
            num_scalar_prefetch=1,
            grid=(1,),
            in_specs=[
                whole((TOK, COLS)), group, group, whole((TOK, HEADS)), whole((HEADS, TOK)), whole((HEADS, TOK)),
                whole((1, HEADS)),
            ],
            out_specs=whole((TOK, COLS)),
        ),
        out_shape=sds((TOK, COLS), F32),
        compiler_params=params,
        cost_estimate=pl.CostEstimate(flops=4 * TOK**3 * HEADS, bytes_accessed=2**21, transcendentals=TOK**2 * HEADS),
        name="mixer_inner",
    )(place, mixer_in, b_proj, c_proj, cum, cumt, stept, skip_gain[None, :])

    half = whole((1, TOK // 2, COLS))
    keep, give = pl.pallas_call(
        finish_kernel,
        grid_spec=pltpu.PrefetchScalarGridSpec(
            num_scalar_prefetch=1,
            grid=(1,),
            in_specs=[
                whole((TOK, COLS)), whole((TOK, COLS)), group, whole((TOK, HEADS)), whole((1, COLS)),
                whole((CTXN, PAY, 128)),
            ],
            out_specs=[half, half],
            scratch_shapes=[pltpu.VMEM((TOK, COLS), F32)],
        ),
        out_shape=[sds((1, TOK // 2, COLS), BF16)] * 2,
        compiler_params=params,
        name="mixer_finish",
    )(place, inner, gate_in, c_proj, cum, norm_gain[None, :], incoming)

    X, Y = ("x_hi", "x_lo"), "y"
    got = moved(give, "core", 1)
    lines = copied(around(keep, X) + around(got, Y), (4, 4), [(k, 0, 1, k // 4, k % 4) for k in range(8)])
    arrays = across(lines[0], Y) + across(lines[1], X)
    terms = jnp.dot(keep[0], w_out, preferred_element_type=F32) + jnp.dot(
        got[0], w_other, preferred_element_type=F32
    )
    (terms, *arrays) = lax.optimization_barrier((terms, *arrays))
    mixed = lax.psum_scatter(terms, ("y", "x_lo"), scatter_dimension=0, tiled=True)

    owned = pattern.reshape(2, 8, 8, 2, 2)[lax.axis_index("x_hi"), :, head_at // 2]
    order = jnp.array(ORDER)
    owned = owned[(lax.axis_index("z") + order) % 8]
    core = lax.axis_index("core")
    where = [where_found(owned[:, (core + k) % 2]) for k in (1, 0)]
    theirs, ours = where
    given3, own3 = make_tiles(jnp.concatenate([theirs[:3], ours[:3]]), arrays, (3, 3), (1,))
    taken3 = moved(given3, "core", 1)
    later, _ = lax.optimization_barrier((theirs[3:], given3))
    (given5,) = make_tiles(later, arrays, (5,), ())

    n = BLK // 2
    four = (own3[0] + taken3[0]).astype(F16)
    own3, taken3 = lax.optimization_barrier((own3, taken3))
    three, five = (own3[k] + taken3[k] for k in (1, 2))
    up, down = moved(four[:n], "z", -1), moved(four[n:], "z", 1)
    up, down, given5, three, five = lax.optimization_barrier((up, down, given5, three, five))
    taken5 = moved(given5, "core", 1)
    (own5,) = make_tiles(ours[3:], arrays, (5,), (0,))

    def tiles(r):
        at = ORDER.index(r) - 3
        return own5[at] + taken5[at]

    up = jnp.concatenate([up.astype(F32) + three[:n], three[n:]], axis=0).astype(F16)
    down = jnp.concatenate([five[:n], down.astype(F32) + five[n:]], axis=0).astype(F16)
    for r in (2, 1):
        up, down = moved(up, "z", -1), moved(down, "z", 1)
        up = (up.astype(F32) + tiles(r)).astype(F16)
        down = (down.astype(F32) + tiles(8 - r)).astype(F16)
    up, down = moved(up, "z", -1), moved(down, "z", 1)
    hessian = (tiles(0) + up.astype(F32) + down.astype(F32)) * (2.0 / 4096 / TILE_SCALE)
    return mixed, hessian[None]


def solution(mesh):
    fine = Mesh(mesh.devices.reshape(2, 8, 4, 2, 2), CTX + HEAD)
    in_specs = (
        P(CTX, HEAD), P(CTX, HEAD), P(CTX, None), P(CTX, None), P(CTX, HEAD), P(HEAD), P(HEAD),
        P(HEAD, None, None), P(HEAD), P(HEAD, None), P(),
    )
    out_specs = (P(CTX + HEAD, None), P(CTX + HEAD, None, None))
    return jax.shard_map(body, mesh=fine, in_specs=in_specs, out_specs=out_specs, check_vma=False)
```

```python
import functools

import jax
import jax.numpy as jnp
from jax import lax
from jax.experimental import pallas as pl
from jax.experimental.pallas import tpu as pltpu
from jax.sharding import Mesh, PartitionSpec as P

G = 8
N = 256
BLK = 512
HEADS = 16
PS = 64
TOK = 256
COLS = HEADS * PS
CTXN = 16
EPS = 1e-05
F32, BF16, F16 = jnp.float32, jnp.bfloat16, jnp.float16
HI = lax.Precision.HIGHEST
XB_MAX = 36.0
ENTER_MAX = 8.0
TINY = 1e-30
TOP = 14.0
LAST = 1000.0
PAY = HEADS // 2 * 16 + 8
ORDER = (4, 3, 5, 2, 6, 1, 7, 0)
VMEM = 24 * 1024 * 1024
SOURCES = 10
TILE_SCALE = 2.0**-8

CTX = ("x_hi", "z")
HEAD = ("y", "x_lo", "core")
ROWS0 = (((0,), (0,)), ((), ()))
ROWS1 = (((1,), (1,)), ((), ()))


def two(v):
    hi = v.astype(BF16)
    return hi, (v - hi.astype(F32)).astype(BF16)


def pair(w, j, lanes):
    return jnp.where(lanes < PS, w[:, 2 * j : 2 * j + 1], w[:, 2 * j + 1 : 2 * j + 2])


def exponent(bound):
    return jnp.clip(jnp.ceil(jnp.log2(jnp.maximum(bound, TINY))) + 1.0, -100.0, 127.0)


def start_kernel(g_ref, x_ref, b_ref, stept_ref, dlog_ref, pay_ref, cum_ref, cumt_ref, hi_ref, lo_ref, extra_ref):
    stept = stept_ref[...]
    own = lax.broadcasted_iota(jnp.int32, (HEADS, HEADS), 0) == lax.broadcasted_iota(jnp.int32, (HEADS, HEADS), 1)
    rate = -jnp.sum(jnp.where(own, jnp.exp(dlog_ref[...]), 0.0), axis=1, keepdims=True)
    logdt = stept * rate
    row = lax.broadcasted_iota(jnp.int32, (TOK, TOK), 0)
    col = lax.broadcasted_iota(jnp.int32, (TOK, TOK), 1)
    cum = lax.dot_general((row >= col).astype(F32), logdt, ROWS1, precision=HI, preferred_element_type=F32)
    cum_ref[...] = cum
    cumt_ref[...] = jnp.dot(logdt, (row <= col).astype(F32), precision=HI, preferred_element_type=F32)
    step = lax.dot_general((row == col).astype(F32), stept, ROWS1, precision=HI, preferred_element_type=F32)
    total = cum[TOK - 1 : TOK, :]
    w = step * jnp.exp(total - cum)
    e = exponent(XB_MAX * jnp.sum(jnp.abs(w), axis=0, keepdims=True))
    total = jnp.clip(total, -LAST, LAST)
    t0 = total.astype(BF16).astype(F32)
    t1 = (total - t0).astype(BF16).astype(F32)
    extra_ref[...] = jnp.zeros((8, 128), F32)
    for i, v in enumerate((t0, t1, total - t0 - t1, e)):
        extra_ref[i : i + 1, :HEADS] = v
    extra = extra_ref[...]
    w = w * jnp.exp2(TOP - e)
    lanes = lax.broadcasted_iota(jnp.int32, (TOK, 128), 1)
    for j in range(HEADS // 2):
        cols = slice(128 * j, 128 * j + 128)
        hi, lo = two(pair(w, j, lanes) * x_ref[:, cols].astype(F32))
        hi_ref[:, cols] = hi
        lo_ref[:, cols] = lo
    b = b_ref[...]
    state = lax.dot_general(b, hi_ref[...], ROWS0, preferred_element_type=F32) + lax.dot_general(
        b, lo_ref[...], ROWS0, preferred_element_type=F32
    )
    for c in range(CTXN):
        for j in range(HEADS // 2):
            pay_ref[c, 16 * j : 16 * j + 16, :] = state[16 * c : 16 * c + 16, 128 * j : 128 * j + 128]
        pay_ref[c, PAY - 8 :, :] = extra


def scan_kernel(at_ref, q_ref, enter_ref, out_ref):
    head = lax.broadcasted_iota(jnp.int32, (128, COLS), 0)
    spread = (lax.broadcasted_iota(jnp.int32, (128, COLS), 1) // PS == head).astype(F32)

    def wide(v):
        return jnp.dot(v, spread, precision=HI, preferred_element_type=F32)

    info = [jnp.concatenate([q_ref[c, PAY - 8 + i : PAY - 7 + i, :] for c in range(CTXN)], axis=0) for i in range(4)]
    d = jnp.exp(info[0] + info[1] + info[2])
    w = jnp.exp2(info[3])
    bounds = [jnp.full((1, 128), ENTER_MAX, F32)]
    for c in range(CTXN - 1):
        bounds.append(d[c : c + 1] * bounds[-1] + w[c : c + 1])
    e = exponent(jnp.concatenate(bounds, axis=0))
    dw, qw, ow = wide(d), wide(jnp.exp2(info[3] - TOP)), wide(jnp.exp2(TOP - e))
    rows = N // CTXN
    mine = lax.broadcasted_iota(jnp.int32, (rows, N), 0) + at_ref[1] * rows
    pick = (lax.broadcasted_iota(jnp.int32, (rows, N), 1) == mine).astype(F32)
    s = lax.dot_general(pick, enter_ref[...], ROWS1, precision=HI, preferred_element_type=F32)
    for j in range(HEADS // 2):
        cols = slice(128 * j, 128 * j + 128)
        here = slice(16 * j, 16 * j + 16)
        sj = s[:, cols]
        for c in range(CTXN):
            out_ref[c, here, :] = sj * ow[c : c + 1, cols]
            sj = dw[c : c + 1, cols] * sj + q_ref[c, here, :] * qw[c : c + 1, cols]
    for c in range(CTXN):
        out_ref[c, PAY - 8 :, :] = jnp.broadcast_to(e[c : c + 1], (8, 128))


def inner_kernel(g_ref, x_ref, b_ref, c_ref, cum_ref, cumt_ref, stept_ref, skip_ref, out_ref):
    scores = lax.dot_general(c_ref[...], b_ref[...], ROWS1, preferred_element_type=F32)
    cum = cum_ref[...]
    skip = skip_ref[...]
    half = TOK // 2
    lanes = lax.broadcasted_iota(jnp.int32, (half, 128), 1)
    for j in range(HEADS // 2):
        cols = slice(128 * j, 128 * j + 128)
        x = x_ref[:, cols]
        for r0, r1 in ((0, half), (half, TOK)):
            row = lax.broadcasted_iota(jnp.int32, (half, r1), 0) + r0
            col = lax.broadcasted_iota(jnp.int32, (half, r1), 1)
            mask = row >= col
            outs = []
            for h in (2 * j, 2 * j + 1):
                differ = cum[r0:r1, h : h + 1] - cumt_ref[h : h + 1, :r1]
                decay = jnp.where(mask, jnp.exp(jnp.where(mask, differ, 0.0)), 0.0)
                hi, lo = two(decay * scores[r0:r1, :r1] * stept_ref[h : h + 1, :r1])
                outs.append(
                    jnp.dot(hi, x[:r1], preferred_element_type=F32) + jnp.dot(lo, x[:r1], preferred_element_type=F32)
                )
            y = jnp.where(lanes < PS, outs[0], outs[1])
            out_ref[r0:r1, cols] = y + pair(skip, j, lanes[:1]) * x[r0:r1].astype(F32)


def finish_kernel(g_ref, y_ref, gate_ref, c_ref, cum_ref, gain_ref, in_ref, keep_ref, give_ref, gated_ref):
    c = c_ref[...]
    carry = jnp.exp(cum_ref[...]) * jnp.exp2(in_ref[0, PAY - 8 : PAY - 7, :HEADS] - TOP)
    half = TOK // 2
    total = jnp.zeros((TOK, 1), F32)
    lanes = lax.broadcasted_iota(jnp.int32, (TOK, 128), 1)
    for j in range(HEADS // 2):
        cols = slice(128 * j, 128 * j + 128)
        hi, lo = two(in_ref[:, 16 * j : 16 * j + 16, :].reshape(N, 128))
        inbound = jnp.dot(c, hi, preferred_element_type=F32) + jnp.dot(c, lo, preferred_element_type=F32)
        y = y_ref[:, cols] + inbound * pair(carry, j, lanes)
        g = gate_ref[:, cols].astype(F32)
        gated = y * (g / (1.0 + jnp.exp(-g)))
        gated_ref[:, cols] = gated
        total = total + jnp.sum(gated * gated, axis=1, keepdims=True)
    scale = lax.rsqrt(total / COLS + EPS)
    features = (gated_ref[...] * scale * gain_ref[...]).reshape(TOK // 32, 2, 16, COLS)
    even, odd = features[:, 0].reshape(half, COLS), features[:, 1].reshape(half, COLS)
    first = g_ref[2] == 0
    keep_ref[0] = jnp.where(first, even, odd).astype(BF16)
    give_ref[0] = jnp.where(first, odd, even).astype(BF16)


def tile_kernel(counts, where_ref, *refs):
    sources, out_refs, (held, sems) = refs[:SOURCES], refs[SOURCES:-2], refs[-2:]
    k, count = pl.program_id(0), pl.num_programs(0)
    places = [(o, x) for o in range(2) for x in range(2)]

    def copy(source, spot, column, slot, place):
        return pltpu.make_async_copy(
            source.at[spot, :, pl.ds(column, BLK)], held.at[(slot,) + place], sems.at[(slot,) + place]
        )

    def start_from(low, high, which, made):
        if high - low == 1:
            made(low).start()
            return
        middle = (low + high) // 2
        pl.when(which < middle)(lambda: start_from(low, middle, which, made))
        pl.when(which >= middle)(lambda: start_from(middle, high, which, made))

    def fetch(tile, slot):
        for n, place in enumerate(places):
            base = (tile * 4 + n) * 3
            which, spot = where_ref[base], where_ref[base + 1]
            column = pl.multiple_of(where_ref[base + 2] * BLK, BLK)
            start_from(0, SOURCES, which, lambda i: copy(sources[i], spot, column, slot, place))

    @pl.when(k == 0)
    def _():
        fetch(0, 0)

    @pl.when(k + 1 < count)
    def _():
        fetch(k + 1, (k + 1) % 2)

    slot = k % 2
    for place in places:
        copy(sources[0], 0, 0, slot, place).wait()
    a = held[slot, 0].reshape(TOK, BLK)
    b = held[slot, 1].reshape(TOK, BLK)
    tile = lax.dot_general(a, b, ROWS0, preferred_element_type=F32) * TILE_SCALE

    at = 0
    for ref, n in zip(out_refs, counts):

        @pl.when((k >= at) & (k < at + n))
        def _(ref=ref):
            ref[0] = tile

        at += n


def whole(shape):
    return pl.BlockSpec(shape, lambda *_: (0,) * len(shape))


def moved(v, axis, by):
    n = lax.axis_size(axis)
    return lax.ppermute(v, axis, [(i, (i - by) % n) for i in range(n)])


def around(v, axis):
    far = moved(v, axis, 2)
    return [v, moved(v, axis, 1), moved(v, axis, -1), far]


def copy_kernel(count, pieces, *refs):
    for a, low, n, o, to in pieces:
        refs[count + o][to : to + n] = refs[a][low : low + n]


def copied(arrays, sizes, pieces):
    shape, dtype = arrays[0].shape[1:], arrays[0].dtype
    return pl.pallas_call(
        functools.partial(copy_kernel, len(arrays), pieces),
        out_shape=[jax.ShapeDtypeStruct((n,) + shape, dtype) for n in sizes],
        compiler_params=pltpu.CompilerParams(vmem_limit_bytes=VMEM),
        cost_estimate=pl.CostEstimate(flops=0, bytes_accessed=2 * sum(sizes) * 2**18, transcendentals=0),
        name="pieces",
    )(*arrays)


def across(line, axis):
    plus, minus = moved(line, axis, 1), moved(line, axis, -1)
    near, rest = copied([plus, minus], (2, 2), ((0, 0, 2, 0, 0), (1, 2, 2, 1, 0)))
    return [line, plus, minus, moved(near, axis, 1), moved(rest, axis, -1)]


def place_of(d):
    d = d % 4
    return jnp.where(d == 2, 3, jnp.where(d == 3, 2, d))


def where_found(blocks):
    head = blocks[:, :, None] // 2
    x = 2 * jnp.arange(2)[None, None, :] + head // 2 % 2
    x = place_of(x - lax.axis_index(("x_hi", "x_lo")))
    y = place_of(head // 4 - lax.axis_index("y")) + 0 * x
    other = (head % 2 != lax.axis_index("core")) + 0 * x
    outer, inner = jnp.where(other == 1, x, y), jnp.where(other == 1, y, x)
    last = (outer == 3) & (inner >= 2)
    found = (outer + last + other * 5, inner - 2 * last, blocks[:, :, None] % 2 + 0 * x)
    return jnp.stack(found, axis=-1).astype(jnp.int32).reshape(blocks.shape[0], 12)


def make_tiles(where, arrays, counts, kept):
    count, at, specs = sum(counts), 0, []
    for n in counts:
        specs.append(pl.BlockSpec((1, BLK, BLK), lambda k, w, at=at, n=n: (jnp.clip(k - at, 0, n - 1), 0, 0)))
        at += n
    return pl.pallas_call(
        functools.partial(tile_kernel, counts),
        grid_spec=pltpu.PrefetchScalarGridSpec(
            num_scalar_prefetch=1,
            grid=(count,),
            in_specs=[pl.BlockSpec(memory_space=pl.ANY)] * SOURCES,
            out_specs=specs,
            scratch_shapes=[pltpu.VMEM((2, 2, 2, TOK // 2, BLK), BF16), pltpu.SemaphoreType.DMA((2, 2, 2))],
        ),
        out_shape=[(jax.ShapeDtypeStruct if n in kept else pltpu.HBM)((counts[n], BLK, BLK), F32) for n in range(len(counts))],
        compiler_params=pltpu.CompilerParams(vmem_limit_bytes=VMEM),
        cost_estimate=pl.CostEstimate(
            flops=count * BLK**3, bytes_accessed=count * 2 * 1024 * 1024, transcendentals=0
        ),
        name="hessian_tiles",
    )(where.reshape(-1), *arrays)


def body(
    mixer_in, gate_in, b_proj, c_proj, step_size, decay_log, skip_gain, entering, norm_gain, w_out, pattern
):
    ctx_at = lax.axis_index(CTX)
    head_at = lax.axis_index(HEAD)
    place = jnp.stack([head_at * HEADS // (256 // G), ctx_at, lax.axis_index("core")]).astype(jnp.int32)
    group = pl.BlockSpec((TOK, N), lambda i, g: (0, g[0]))
    params = pltpu.CompilerParams(vmem_limit_bytes=VMEM)
    sds = jax.ShapeDtypeStruct

    stept = step_size.T
    sent, cum, cumt = pl.pallas_call(
        start_kernel,
        grid_spec=pltpu.PrefetchScalarGridSpec(
            num_scalar_prefetch=1,
            grid=(1,),
            in_specs=[whole((TOK, COLS)), group, whole((HEADS, TOK)), whole((1, HEADS))],
            out_specs=[whole((CTXN, PAY, 128)), whole((TOK, HEADS)), whole((HEADS, TOK))],
            scratch_shapes=[pltpu.VMEM((TOK, COLS), BF16)] * 2 + [pltpu.VMEM((8, 128), F32)],
        ),
        out_shape=[sds((CTXN, PAY, 128), F32), sds((TOK, HEADS), F32), sds((HEADS, TOK), F32)],
        compiler_params=params,
        name="mixer_start",
    )(place, mixer_in, b_proj, stept, decay_log[None, :])

    w_other = moved(w_out, "core", 1)
    sent = lax.all_to_all(sent.astype(F16), CTX, 0, 0, tiled=True)
    sent, w_other = lax.optimization_barrier((sent, w_other))
    sent = sent.astype(F32)
    incoming = pl.pallas_call(
        scan_kernel,
        grid_spec=pltpu.PrefetchScalarGridSpec(
            num_scalar_prefetch=1,
            grid=(1,),
            in_specs=[whole((CTXN, PAY, 128)), whole((COLS, N))],
            out_specs=whole((CTXN, PAY, 128)),
        ),
        out_shape=sds((CTXN, PAY, 128), F32),
        compiler_params=params,
        name="state_scan",
    )(place, sent, entering.reshape(COLS, N))
    incoming = lax.all_to_all(incoming.astype(F16), CTX, 0, 0, tiled=True).astype(F32)

    inner = pl.pallas_call(
        inner_kernel,
        grid_spec=pltpu.PrefetchScalarGridSpec(
            num_scalar_prefetch=1,
            grid=(1,),
            in_specs=[
                whole((TOK, COLS)), group, group, whole((TOK, HEADS)), whole((HEADS, TOK)), whole((HEADS, TOK)),
                whole((1, HEADS)),
            ],
            out_specs=whole((TOK, COLS)),
        ),
        out_shape=sds((TOK, COLS), F32),
        compiler_params=params,
        cost_estimate=pl.CostEstimate(flops=4 * TOK**3 * HEADS, bytes_accessed=2**21, transcendentals=TOK**2 * HEADS),
        name="mixer_inner",
    )(place, mixer_in, b_proj, c_proj, cum, cumt, stept, skip_gain[None, :])

    half = whole((1, TOK // 2, COLS))
    keep, give = pl.pallas_call(
        finish_kernel,
        grid_spec=pltpu.PrefetchScalarGridSpec(
            num_scalar_prefetch=1,
            grid=(1,),
            in_specs=[
                whole((TOK, COLS)), whole((TOK, COLS)), group, whole((TOK, HEADS)), whole((1, COLS)),
                whole((CTXN, PAY, 128)),
            ],
            out_specs=[half, half],
            scratch_shapes=[pltpu.VMEM((TOK, COLS), F32)],
        ),
        out_shape=[sds((1, TOK // 2, COLS), BF16)] * 2,
        compiler_params=params,
        name="mixer_finish",
    )(place, inner, gate_in, c_proj, cum, norm_gain[None, :], incoming)

    X, Y = ("x_hi", "x_lo"), "y"
    got = moved(give, "core", 1)
    lines = copied(around(keep, X) + around(got, Y), (4, 4), [(k, 0, 1, k // 4, k % 4) for k in range(8)])
    arrays = across(lines[0], Y) + across(lines[1], X)
    terms = jnp.dot(keep[0], w_out, preferred_element_type=F32) + jnp.dot(
        got[0], w_other, preferred_element_type=F32
    )
    (terms, *arrays) = lax.optimization_barrier((terms, *arrays))
    mixed = lax.psum_scatter(terms, ("y", "x_lo"), scatter_dimension=0, tiled=True)

    owned = pattern.reshape(2, 8, 8, 2, 2)[lax.axis_index("x_hi"), :, head_at // 2]
    order = jnp.array(ORDER)
    owned = owned[(lax.axis_index("z") + order) % 8]
    core = lax.axis_index("core")
    where = [where_found(owned[:, (core + k) % 2]) for k in (1, 0)]
    theirs, ours = where
    (given3,) = make_tiles(theirs[:3], arrays, (3,), ())
    later, given3 = lax.optimization_barrier((ours[:3], given3))
    taken3 = moved(given3, "core", 1)
    (own3,) = make_tiles(later, arrays, (3,), ())
    four = (own3[0] + taken3[0]).astype(F16)
    four, own3, taken3 = lax.optimization_barrier((four, own3, taken3))

    n = BLK // 2
    up, down = moved(four[:n], "z", -1), moved(four[n:], "z", 1)
    three, five = (own3[k] + taken3[k] for k in (1, 2))
    beside = (three.astype(F16), five.astype(F16))
    later, beside = lax.optimization_barrier((theirs[3:], beside))
    (given5,) = make_tiles(later, arrays, (5,), ())
    up, down, given5, beside = lax.optimization_barrier((up, down, given5, beside))
    taken5 = moved(given5, "core", 1)
    (own5,) = make_tiles(ours[3:], arrays, (5,), (0,))
    two_ways = [(own5, taken5), lax.optimization_barrier((own5, taken5))]

    def tiles(r):
        at = ORDER.index(r) - 3
        own, taken = two_ways[r > 4]
        return own[at] + taken[at]

    up = up.astype(F32) + own3[1, :n] + taken3[1, :n]
    down = down.astype(F32) + own3[2, n:] + taken3[2, n:]
    up = lax.dynamic_update_slice(beside[0], up.astype(F16), (0, 0))
    down = lax.dynamic_update_slice(beside[1], down.astype(F16), (n, 0))
    for r in (2, 1):
        up, down = moved(up, "z", -1), moved(down, "z", 1)
        up = (up.astype(F32) + tiles(r)).astype(F16)
        down = (down.astype(F32) + tiles(8 - r)).astype(F16)
    up, down = moved(up, "z", -1), moved(down, "z", 1)
    hessian = (tiles(0) + up.astype(F32) + down.astype(F32)) * (2.0 / 4096 / TILE_SCALE)
    return mixed, hessian[None]


def solution(mesh):
    fine = Mesh(mesh.devices.reshape(2, 8, 4, 2, 2), CTX + HEAD)
    in_specs = (
        P(CTX, HEAD), P(CTX, HEAD), P(CTX, None), P(CTX, None), P(CTX, HEAD), P(HEAD), P(HEAD),
        P(HEAD, None, None), P(HEAD), P(HEAD, None), P(),
    )
    out_specs = (P(CTX + HEAD, None), P(CTX + HEAD, None, None))
    return jax.shard_map(body, mesh=fine, in_specs=in_specs, out_specs=out_specs, check_vma=False)
```

```python
import functools

import jax
import jax.numpy as jnp
from jax import lax
from jax.experimental import pallas as pl
from jax.experimental.pallas import tpu as pltpu
from jax.sharding import Mesh, PartitionSpec as P

G = 8
N = 256
BLK = 512
HEADS = 16
PS = 64
TOK = 256
COLS = HEADS * PS
CTXN = 16
EPS = 1e-05
F32, BF16, F16 = jnp.float32, jnp.bfloat16, jnp.float16
HI = lax.Precision.HIGHEST
XB_MAX = 36.0
ENTER_MAX = 8.0
TINY = 1e-30
TOP = 14.0
LAST = 1000.0
PAY = HEADS // 2 * 16 + 8
ORDER = (4, 3, 5, 2, 6, 1, 7, 0)
VMEM = 16 * 1024 * 1024
SOURCES = 10
TILE_SCALE = 2.0**-8

CTX = ("x_hi", "z")
HEAD = ("y", "x_lo", "core")
ROWS0 = (((0,), (0,)), ((), ()))
ROWS1 = (((1,), (1,)), ((), ()))


def two(v):
    hi = v.astype(BF16)
    return hi, (v - hi.astype(F32)).astype(BF16)


def pair(w, j, lanes):
    return jnp.where(lanes < PS, w[:, 2 * j : 2 * j + 1], w[:, 2 * j + 1 : 2 * j + 2])


def exponent(bound):
    return jnp.clip(jnp.ceil(jnp.log2(jnp.maximum(bound, TINY))) + 1.0, -100.0, 127.0)


def start_kernel(g_ref, x_ref, b_ref, stept_ref, dlog_ref, pay_ref, cum_ref, cumt_ref, hi_ref, lo_ref, extra_ref):
    stept = stept_ref[...]
    own = lax.broadcasted_iota(jnp.int32, (HEADS, HEADS), 0) == lax.broadcasted_iota(jnp.int32, (HEADS, HEADS), 1)
    rate = -jnp.sum(jnp.where(own, jnp.exp(dlog_ref[...]), 0.0), axis=1, keepdims=True)
    logdt = stept * rate
    row = lax.broadcasted_iota(jnp.int32, (TOK, TOK), 0)
    col = lax.broadcasted_iota(jnp.int32, (TOK, TOK), 1)
    cum = lax.dot_general((row >= col).astype(F32), logdt, ROWS1, precision=HI, preferred_element_type=F32)
    cum_ref[...] = cum
    cumt_ref[...] = jnp.dot(logdt, (row <= col).astype(F32), precision=HI, preferred_element_type=F32)
    step = lax.dot_general((row == col).astype(F32), stept, ROWS1, precision=HI, preferred_element_type=F32)
    total = cum[TOK - 1 : TOK, :]
    w = step * jnp.exp(total - cum)
    e = exponent(XB_MAX * jnp.sum(jnp.abs(w), axis=0, keepdims=True))
    total = jnp.clip(total, -LAST, LAST)
    t0 = total.astype(BF16).astype(F32)
    t1 = (total - t0).astype(BF16).astype(F32)
    extra_ref[...] = jnp.zeros((8, 128), F32)
    for i, v in enumerate((t0, t1, total - t0 - t1, e)):
        extra_ref[i : i + 1, :HEADS] = v
    extra = extra_ref[...]
    w = w * jnp.exp2(TOP - e)
    lanes = lax.broadcasted_iota(jnp.int32, (TOK, 128), 1)
    for j in range(HEADS // 2):
        cols = slice(128 * j, 128 * j + 128)
        hi, lo = two(pair(w, j, lanes) * x_ref[:, cols].astype(F32))
        hi_ref[:, cols] = hi
        lo_ref[:, cols] = lo
    b = b_ref[...]
    state = lax.dot_general(b, hi_ref[...], ROWS0, preferred_element_type=F32) + lax.dot_general(
        b, lo_ref[...], ROWS0, preferred_element_type=F32
    )
    for c in range(CTXN):
        for j in range(HEADS // 2):
            pay_ref[c, 16 * j : 16 * j + 16, :] = state[16 * c : 16 * c + 16, 128 * j : 128 * j + 128]
        pay_ref[c, PAY - 8 :, :] = extra


def scan_kernel(at_ref, q_ref, enter_ref, out_ref):
    head = lax.broadcasted_iota(jnp.int32, (128, COLS), 0)
    spread = (lax.broadcasted_iota(jnp.int32, (128, COLS), 1) // PS == head).astype(F32)

    def wide(v):
        return jnp.dot(v, spread, precision=HI, preferred_element_type=F32)

    info = [jnp.concatenate([q_ref[c, PAY - 8 + i : PAY - 7 + i, :] for c in range(CTXN)], axis=0) for i in range(4)]
    d = jnp.exp(info[0] + info[1] + info[2])
    w = jnp.exp2(info[3])
    bounds = [jnp.full((1, 128), ENTER_MAX, F32)]
    for c in range(CTXN - 1):
        bounds.append(d[c : c + 1] * bounds[-1] + w[c : c + 1])
    e = exponent(jnp.concatenate(bounds, axis=0))
    dw, qw, ow = wide(d), wide(jnp.exp2(info[3] - TOP)), wide(jnp.exp2(TOP - e))
    rows = N // CTXN
    mine = lax.broadcasted_iota(jnp.int32, (rows, N), 0) + at_ref[1] * rows
    pick = (lax.broadcasted_iota(jnp.int32, (rows, N), 1) == mine).astype(F32)
    s = lax.dot_general(pick, enter_ref[...], ROWS1, precision=HI, preferred_element_type=F32)
    for j in range(HEADS // 2):
        cols = slice(128 * j, 128 * j + 128)
        here = slice(16 * j, 16 * j + 16)
        sj = s[:, cols]
        for c in range(CTXN):
            out_ref[c, here, :] = sj * ow[c : c + 1, cols]
            sj = dw[c : c + 1, cols] * sj + q_ref[c, here, :] * qw[c : c + 1, cols]
    for c in range(CTXN):
        out_ref[c, PAY - 8 :, :] = jnp.broadcast_to(e[c : c + 1], (8, 128))


def inner_kernel(g_ref, x_ref, b_ref, c_ref, cum_ref, cumt_ref, stept_ref, skip_ref, out_ref):
    scores = lax.dot_general(c_ref[...], b_ref[...], ROWS1, preferred_element_type=F32)
    cum = cum_ref[...]
    skip = skip_ref[...]
    half = TOK // 2
    lanes = lax.broadcasted_iota(jnp.int32, (half, 128), 1)
    for j in range(HEADS // 2):
        cols = slice(128 * j, 128 * j + 128)
        x = x_ref[:, cols]
        for r0, r1 in ((0, half), (half, TOK)):
            row = lax.broadcasted_iota(jnp.int32, (half, r1), 0) + r0
            col = lax.broadcasted_iota(jnp.int32, (half, r1), 1)
            mask = row >= col
            outs = []
            for h in (2 * j, 2 * j + 1):
                differ = cum[r0:r1, h : h + 1] - cumt_ref[h : h + 1, :r1]
                decay = jnp.where(mask, jnp.exp(jnp.where(mask, differ, 0.0)), 0.0)
                hi, lo = two(decay * scores[r0:r1, :r1] * stept_ref[h : h + 1, :r1])
                outs.append(
                    jnp.dot(hi, x[:r1], preferred_element_type=F32) + jnp.dot(lo, x[:r1], preferred_element_type=F32)
                )
            y = jnp.where(lanes < PS, outs[0], outs[1])
            out_ref[r0:r1, cols] = y + pair(skip, j, lanes[:1]) * x[r0:r1].astype(F32)


def finish_kernel(g_ref, y_ref, gate_ref, c_ref, cum_ref, gain_ref, in_ref, keep_ref, give_ref, gated_ref):
    c = c_ref[...]
    carry = jnp.exp(cum_ref[...]) * jnp.exp2(in_ref[0, PAY - 8 : PAY - 7, :HEADS] - TOP)
    half = TOK // 2
    total = jnp.zeros((TOK, 1), F32)
    lanes = lax.broadcasted_iota(jnp.int32, (TOK, 128), 1)
    for j in range(HEADS // 2):
        cols = slice(128 * j, 128 * j + 128)
        hi, lo = two(in_ref[:, 16 * j : 16 * j + 16, :].reshape(N, 128))
        inbound = jnp.dot(c, hi, preferred_element_type=F32) + jnp.dot(c, lo, preferred_element_type=F32)
        y = y_ref[:, cols] + inbound * pair(carry, j, lanes)
        g = gate_ref[:, cols].astype(F32)
        gated = y * (g / (1.0 + jnp.exp(-g)))
        gated_ref[:, cols] = gated
        total = total + jnp.sum(gated * gated, axis=1, keepdims=True)
    scale = lax.rsqrt(total / COLS + EPS)
    features = (gated_ref[...] * scale * gain_ref[...]).reshape(TOK // 32, 2, 16, COLS)
    even, odd = features[:, 0].reshape(half, COLS), features[:, 1].reshape(half, COLS)
    first = g_ref[2] == 0
    keep_ref[0] = jnp.where(first, even, odd).astype(BF16)
    give_ref[0] = jnp.where(first, odd, even).astype(BF16)


def tile_kernel(counts, where_ref, *refs):
    sources, out_refs, (held, sems) = refs[:SOURCES], refs[SOURCES:-2], refs[-2:]
    k, count = pl.program_id(0), pl.num_programs(0)
    places = [(o, x) for o in range(2) for x in range(2)]

    def copy(source, spot, column, slot, place):
        return pltpu.make_async_copy(
            source.at[spot, :, pl.ds(column, BLK)], held.at[(slot,) + place], sems.at[(slot,) + place]
        )

    def start_from(low, high, which, made):
        if high - low == 1:
            made(low).start()
            return
        middle = (low + high) // 2
        pl.when(which < middle)(lambda: start_from(low, middle, which, made))
        pl.when(which >= middle)(lambda: start_from(middle, high, which, made))

    def fetch(tile, slot):
        for n, place in enumerate(places):
            base = (tile * 4 + n) * 3
            which, spot = where_ref[base], where_ref[base + 1]
            column = pl.multiple_of(where_ref[base + 2] * BLK, BLK)
            start_from(0, SOURCES, which, lambda i: copy(sources[i], spot, column, slot, place))

    @pl.when(k == 0)
    def _():
        fetch(0, 0)

    @pl.when(k + 1 < count)
    def _():
        fetch(k + 1, (k + 1) % 2)

    slot = k % 2
    for place in places:
        copy(sources[0], 0, 0, slot, place).wait()
    a = held[slot, 0].reshape(TOK, BLK)
    b = held[slot, 1].reshape(TOK, BLK)
    tile = lax.dot_general(a, b, ROWS0, preferred_element_type=F32) * TILE_SCALE

    at = 0
    for ref, n in zip(out_refs, counts):

        @pl.when((k >= at) & (k < at + n))
        def _(ref=ref):
            ref[0] = tile

        at += n


def whole(shape):
    return pl.BlockSpec(shape, lambda *_: (0,) * len(shape))


def moved(v, axis, by):
    n = lax.axis_size(axis)
    return lax.ppermute(v, axis, [(i, (i - by) % n) for i in range(n)])


def around(v, axis):
    far = moved(v, axis, 2)
    return [v, moved(v, axis, 1), moved(v, axis, -1), far]


def copy_kernel(count, pieces, *refs):
    for a, low, n, o, to in pieces:
        refs[count + o][to : to + n] = refs[a][low : low + n]


def copied(arrays, sizes, pieces):
    shape, dtype = arrays[0].shape[1:], arrays[0].dtype
    return pl.pallas_call(
        functools.partial(copy_kernel, len(arrays), pieces),
        out_shape=[jax.ShapeDtypeStruct((n,) + shape, dtype) for n in sizes],
        compiler_params=pltpu.CompilerParams(vmem_limit_bytes=VMEM),
        cost_estimate=pl.CostEstimate(flops=0, bytes_accessed=2 * sum(sizes) * 2**18, transcendentals=0),
        name="pieces",
    )(*arrays)


def across(line, axis):
    plus, minus = moved(line, axis, 1), moved(line, axis, -1)
    near, rest = copied([plus, minus], (2, 2), ((0, 0, 2, 0, 0), (1, 2, 2, 1, 0)))
    return [line, plus, minus, moved(near, axis, 1), moved(rest, axis, -1)]


def place_of(d):
    d = d % 4
    return jnp.where(d == 2, 3, jnp.where(d == 3, 2, d))


def where_found(blocks):
    head = blocks[:, :, None] // 2
    x = 2 * jnp.arange(2)[None, None, :] + head // 2 % 2
    x = place_of(x - lax.axis_index(("x_hi", "x_lo")))
    y = place_of(head // 4 - lax.axis_index("y")) + 0 * x
    other = (head % 2 != lax.axis_index("core")) + 0 * x
    outer, inner = jnp.where(other == 1, x, y), jnp.where(other == 1, y, x)
    last = (outer == 3) & (inner >= 2)
    found = (outer + last + other * 5, inner - 2 * last, blocks[:, :, None] % 2 + 0 * x)
    return jnp.stack(found, axis=-1).astype(jnp.int32).reshape(blocks.shape[0], 12)


def make_tiles(where, arrays, counts, kept):
    count, at, specs = sum(counts), 0, []
    for n in counts:
        specs.append(pl.BlockSpec((1, BLK, BLK), lambda k, w, at=at, n=n: (jnp.clip(k - at, 0, n - 1), 0, 0)))
        at += n
    return pl.pallas_call(
        functools.partial(tile_kernel, counts),
        grid_spec=pltpu.PrefetchScalarGridSpec(
            num_scalar_prefetch=1,
            grid=(count,),
            in_specs=[pl.BlockSpec(memory_space=pl.ANY)] * SOURCES,
            out_specs=specs,
            scratch_shapes=[pltpu.VMEM((2, 2, 2, TOK // 2, BLK), BF16), pltpu.SemaphoreType.DMA((2, 2, 2))],
        ),
        out_shape=[(jax.ShapeDtypeStruct if n in kept else pltpu.HBM)((counts[n], BLK, BLK), F32) for n in range(len(counts))],
        compiler_params=pltpu.CompilerParams(vmem_limit_bytes=VMEM),
        cost_estimate=pl.CostEstimate(
            flops=count * BLK**3, bytes_accessed=count * 2 * 1024 * 1024, transcendentals=0
        ),
        name="hessian_tiles",
    )(where.reshape(-1), *arrays)


def body(
    mixer_in, gate_in, b_proj, c_proj, step_size, decay_log, skip_gain, entering, norm_gain, w_out, pattern
):
    ctx_at = lax.axis_index(CTX)
    head_at = lax.axis_index(HEAD)
    place = jnp.stack([head_at * HEADS // (256 // G), ctx_at, lax.axis_index("core")]).astype(jnp.int32)
    group = pl.BlockSpec((TOK, N), lambda i, g: (0, g[0]))
    params = pltpu.CompilerParams(vmem_limit_bytes=VMEM)
    sds = jax.ShapeDtypeStruct

    stept = step_size.T
    sent, cum, cumt = pl.pallas_call(
        start_kernel,
        grid_spec=pltpu.PrefetchScalarGridSpec(
            num_scalar_prefetch=1,
            grid=(1,),
            in_specs=[whole((TOK, COLS)), group, whole((HEADS, TOK)), whole((1, HEADS))],
            out_specs=[whole((CTXN, PAY, 128)), whole((TOK, HEADS)), whole((HEADS, TOK))],
            scratch_shapes=[pltpu.VMEM((TOK, COLS), BF16)] * 2 + [pltpu.VMEM((8, 128), F32)],
        ),
        out_shape=[sds((CTXN, PAY, 128), F32), sds((TOK, HEADS), F32), sds((HEADS, TOK), F32)],
        compiler_params=params,
        name="mixer_start",
    )(place, mixer_in, b_proj, stept, decay_log[None, :])

    w_other = moved(w_out, "core", 1)
    sent = lax.all_to_all(sent.astype(F16), CTX, 0, 0, tiled=True)
    sent, w_other = lax.optimization_barrier((sent, w_other))
    sent = sent.astype(F32)
    incoming = pl.pallas_call(
        scan_kernel,
        grid_spec=pltpu.PrefetchScalarGridSpec(
            num_scalar_prefetch=1,
            grid=(1,),
            in_specs=[whole((CTXN, PAY, 128)), whole((COLS, N))],
            out_specs=whole((CTXN, PAY, 128)),
        ),
        out_shape=sds((CTXN, PAY, 128), F32),
        compiler_params=params,
        name="state_scan",
    )(place, sent, entering.reshape(COLS, N))
    incoming = lax.all_to_all(incoming.astype(F16), CTX, 0, 0, tiled=True).astype(F32)

    inner = pl.pallas_call(
        inner_kernel,
        grid_spec=pltpu.PrefetchScalarGridSpec(
            num_scalar_prefetch=1,
            grid=(1,),
            in_specs=[
                whole((TOK, COLS)), group, group, whole((TOK, HEADS)), whole((HEADS, TOK)), whole((HEADS, TOK)),
                whole((1, HEADS)),
            ],
            out_specs=whole((TOK, COLS)),
        ),
        out_shape=sds((TOK, COLS), F32),
        compiler_params=params,
        cost_estimate=pl.CostEstimate(flops=4 * TOK**3 * HEADS, bytes_accessed=2**21, transcendentals=TOK**2 * HEADS),
        name="mixer_inner",
    )(place, mixer_in, b_proj, c_proj, cum, cumt, stept, skip_gain[None, :])

    half = whole((1, TOK // 2, COLS))
    keep, give = pl.pallas_call(
        finish_kernel,
        grid_spec=pltpu.PrefetchScalarGridSpec(
            num_scalar_prefetch=1,
            grid=(1,),
            in_specs=[
                whole((TOK, COLS)), whole((TOK, COLS)), group, whole((TOK, HEADS)), whole((1, COLS)),
                whole((CTXN, PAY, 128)),
            ],
            out_specs=[half, half],
            scratch_shapes=[pltpu.VMEM((TOK, COLS), F32)],
        ),
        out_shape=[sds((1, TOK // 2, COLS), BF16)] * 2,
        compiler_params=params,
        name="mixer_finish",
    )(place, inner, gate_in, c_proj, cum, norm_gain[None, :], incoming)

    X, Y = ("x_hi", "x_lo"), "y"
    got = moved(give, "core", 1)
    lines = copied(around(keep, X) + around(got, Y), (4, 4), [(k, 0, 1, k // 4, k % 4) for k in range(8)])
    arrays = across(lines[0], Y) + across(lines[1], X)
    terms = jnp.dot(keep[0], w_out, preferred_element_type=F32) + jnp.dot(
        got[0], w_other, preferred_element_type=F32
    )
    (terms, *arrays) = lax.optimization_barrier((terms, *arrays))
    mixed = lax.psum_scatter(terms, ("y", "x_lo"), scatter_dimension=0, tiled=True)

    owned = pattern.reshape(2, 8, 8, 2, 2)[lax.axis_index("x_hi"), :, head_at // 2]
    order = jnp.array(ORDER)
    owned = owned[(lax.axis_index("z") + order) % 8]
    core = lax.axis_index("core")
    where = [where_found(owned[:, (core + k) % 2]) for k in (1, 0)]
    theirs, ours = where
    (given3,) = make_tiles(theirs[:3], arrays, (3,), ())
    later, given3 = lax.optimization_barrier((ours[:3], given3))
    taken3 = moved(given3, "core", 1)
    (own3,) = make_tiles(later, arrays, (3,), ())
    four = (own3[0] + taken3[0]).astype(F16)
    four, own3, taken3 = lax.optimization_barrier((four, own3, taken3))

    n = BLK // 2
    up, down = moved(four[:n], "z", -1), moved(four[n:], "z", 1)
    three, five = (own3[k] + taken3[k] for k in (1, 2))
    beside = (three.astype(F16), five.astype(F16))
    later, beside = lax.optimization_barrier((theirs[3:], beside))
    (given5,) = make_tiles(later, arrays, (5,), ())
    up, down, given5, beside = lax.optimization_barrier((up, down, given5, beside))
    taken5 = moved(given5, "core", 1)
    (own5,) = make_tiles(ours[3:], arrays, (5,), (0,))
    two_ways = [(own5, taken5), lax.optimization_barrier((own5, taken5))]

    def tiles(r):
        at = ORDER.index(r) - 3
        own, taken = two_ways[r > 4]
        return own[at] + taken[at]

    up = up.astype(F32) + own3[1, :n] + taken3[1, :n]
    down = down.astype(F32) + own3[2, n:] + taken3[2, n:]
    up = lax.dynamic_update_slice(beside[0], up.astype(F16), (0, 0))
    down = lax.dynamic_update_slice(beside[1], down.astype(F16), (n, 0))
    for r in (2, 1):
        up, down = moved(up, "z", -1), moved(down, "z", 1)
        up = (up.astype(F32) + tiles(r)).astype(F16)
        down = (down.astype(F32) + tiles(8 - r)).astype(F16)
    up, down = moved(up, "z", -1), moved(down, "z", 1)
    hessian = (tiles(0) + up.astype(F32) + down.astype(F32)) * (2.0 / 4096 / TILE_SCALE)
    return mixed, hessian[None]


def solution(mesh):
    fine = Mesh(mesh.devices.reshape(2, 8, 4, 2, 2), CTX + HEAD)
    in_specs = (
        P(CTX, HEAD), P(CTX, HEAD), P(CTX, None), P(CTX, None), P(CTX, HEAD), P(HEAD), P(HEAD),
        P(HEAD, None, None), P(HEAD), P(HEAD, None), P(),
    )
    out_specs = (P(CTX + HEAD, None), P(CTX + HEAD, None, None))
    return jax.shard_map(body, mesh=fine, in_specs=in_specs, out_specs=out_specs, check_vma=False)
```
